512 devices in a mesh: ctx: 64 (over x, z_hi, y), tp: 8 (over z_lo, core).
Axes of the slice: x: 4, y: 4, z: 16 (z_hi: 4, z_lo: 4; z = z_hi * 4 + z_lo), core: 2. Of those that a mesh axis runs over, the one named last changes fastest.
Arguments:
- query_branch: bfloat16 [12288, 2048], P('ctx', 'tp'), may hold values from -6 to 6
- key_branch: bfloat16 [12288, 2048], P('ctx', 'tp'), may hold values from -6 to 6
- value_branch: bfloat16 [12288, 2048], P('ctx', 'tp'), may hold values from -6 to 6
- spectrum: float32 [2, 128, 192, 2048], P(None, 'ctx', None, 'tp'), may hold values from -6 to 6
- skip_gain: float32 [2048], P('tp'), may hold values from -4 to 4
- out_weight: bfloat16 [2048, 4096], P('tp'), may hold values from -0.125 to 0.125
Outputs:
- layer_out: bfloat16 [12288, 4096], P('ctx', 'tp')
The draws below stay inside these ranges and needn't reach their ends.
All inputs are finite; a program needn't handle non-finite values.
Results may differ from the reference program's by a relative error of at most 0.017.
Values may be sent and summed in bfloat16 or wider, within the bound.
No kernel may reach another device: no remote copies, remote signals or barrier semaphores. Data moves between devices by JAX's collectives and lax.ppermute only.
A program may use at most 64 MiB of HBM per device.

```python
import jax
import jax.numpy as jnp
from jax import lax

D = 4096
C = 2048
TOK_DEV = 192
SEQ = 12288
ROWS = 128
FFTLEN = 24576
N_TP = 8


def block_levels(stream_key, shape, cuts, smallest, top_value):
    gain, own = 1.0, jax.random.fold_in(stream_key, 6)
    for dim, shards_of in cuts:
        heights = jnp.exp(jax.random.uniform(jax.random.fold_in(own, dim), (shards_of,), jnp.float32, smallest / len(cuts), top_value / len(cuts)))
        gain = gain * jnp.repeat(heights, shape[dim] // shards_of).reshape([-1 if axis == dim else 1 for axis in range(len(shape))])
    return gain


def centred(stream_key, dims, spread, limit, split=(), dtype=jnp.bfloat16):
    values = jax.random.normal(stream_key, dims, jnp.float32) * spread
    if len(split) > 0:
        values = block_levels(stream_key, dims, split, -0.22, 0.18) * values
    return jnp.clip(values, min=-limit, max=limit).astype(dtype)


def setup_inputs(seed: int = 0) -> dict:
    arg_keys = jax.random.split(jax.random.key(seed), 7)
    query_branch = centred(arg_keys[0], (SEQ, C), 1.0, 6.0, ((0, 64), (1, 8)))
    key_branch = centred(arg_keys[1], (SEQ, C), 1.0, 6.0, ((0, 64), (1, 8)))
    value_branch = centred(arg_keys[2], (SEQ, C), 1.0, 6.0, ((0, 64), (1, 8)))
    spectrum = centred(arg_keys[3], (2, ROWS, TOK_DEV, C), 1.0, 6.0, ((1, 64), (3, 8)), jnp.float32)
    skip_gain = centred(arg_keys[4], (C,), 1.0, 4.0, ((0, 8),), jnp.float32)
    out_weight = centred(arg_keys[5], (C, D), C ** -0.5, 0.125, ((0, 8),))
    return dict(query_branch=query_branch, key_branch=key_branch, value_branch=value_branch, spectrum=spectrum, skip_gain=skip_gain, out_weight=out_weight)


def reference(query_branch, key_branch, value_branch, spectrum, skip_gain, out_weight):
    mixed_in = (key_branch.astype(jnp.float32) * value_branch.astype(jnp.float32)).astype(jnp.bfloat16)
    signal = mixed_in.astype(jnp.float32)
    block_width = 128 if C % 128 == 0 else C
    block_count = C // block_width
    natural_spectrum = jnp.transpose(spectrum, (0, 2, 1, 3)).reshape(2, FFTLEN, block_count, block_width)
    spectrum_blocks = jnp.transpose(natural_spectrum, (2, 0, 1, 3))
    signal_blocks = jnp.transpose(signal.reshape(SEQ, block_count, block_width), (1, 0, 2))

    def convolve_block(pair):
        signal_block, filter_block = pair
        forward = jnp.fft.fft(signal_block, n=FFTLEN, axis=0)
        product = forward * (filter_block[0] + 1j * filter_block[1])
        inverse = jnp.fft.ifft(product, axis=0)
        return jnp.real(inverse[:SEQ])

    convolved = lax.map(convolve_block, (signal_blocks, spectrum_blocks))
    convolved = jnp.transpose(convolved, (1, 0, 2)).reshape(SEQ, C)
    gated_out = (query_branch.astype(jnp.float32) * (convolved + skip_gain * signal)).astype(jnp.bfloat16)
    slice_width = C // N_TP

    def add_partial(index, summed):
        first = (index * slice_width).astype(jnp.int32)
        gated_block = lax.dynamic_slice_in_dim(gated_out, first, slice_width, 1)
        weight_rows = lax.dynamic_slice_in_dim(out_weight, first, slice_width, 0)
        partial_sum = jnp.dot(gated_block, weight_rows, preferred_element_type=jnp.float32).astype(jnp.bfloat16)
        partial_sum = lax.optimization_barrier(partial_sum)
        return summed + partial_sum.astype(jnp.float32)

    summed = lax.fori_loop(0, N_TP, add_partial, jnp.zeros((SEQ, D), jnp.float32))
    return summed.astype(jnp.bfloat16)
```

```python
import math

import jax
import jax.numpy as jnp
import numpy as np
from jax import lax
from jax.sharding import Mesh
from jax.sharding import PartitionSpec as P

CTX = ("x", "zh", "y")
TP = ("zl", "core")


def tables(groups, tokens):
    rows = 2 * groups
    local = rows // groups
    length = rows * tokens
    kb = (np.arange(local)[:, None] + local * np.arange(groups)[None, :]).reshape(-1)
    n1 = np.arange(groups)
    n2 = np.arange(tokens)
    first = 2.0 * math.pi * (np.outer(kb, n1) % rows) / rows
    middle = 2.0 * math.pi * (np.outer(n2, n2) % tokens) / tokens
    turn = 2.0 * math.pi * (np.outer(kb, n2) % length) / length
    fwd = np.concatenate([np.cos(first), -np.sin(first)], axis=0)
    back = np.concatenate([np.cos(first), -np.sin(first)], axis=0).T / length
    cos_m, sin_m = np.cos(middle), np.sin(middle)
    mid = np.block([[cos_m, -sin_m], [sin_m, cos_m]])
    return fwd, back, mid, np.cos(turn), np.sin(turn)


def bf(values):
    return jnp.asarray(values, jnp.bfloat16)


def dot(a, b, dims):
    return lax.dot_general(a, b, (dims, ((), ())), preferred_element_type=jnp.float32)


def convolve(signal, filt):
    groups, chans, tokens = signal.shape
    fwd, back, mid, tc, ts = tables(groups, tokens)
    rows = 2 * groups
    tc = jnp.asarray(tc, jnp.float32)[:, None, :]
    ts = jnp.asarray(ts, jnp.float32)[:, None, :]
    a = dot(bf(fwd), signal.reshape(groups, -1), ((1,), (0,)))
    a = a.reshape(2, rows, chans, tokens)
    are, aim = a[0] * tc + a[1] * ts, a[1] * tc - a[0] * ts
    a = jnp.concatenate([are, aim], axis=-1).astype(jnp.bfloat16)
    b = dot(a, bf(mid), ((2,), (0,)))
    bre, bim = b[..., :tokens], b[..., tokens:]
    h = filt.transpose(2, 3, 0, 1, 4).reshape(2, rows, chans, tokens).astype(jnp.float32)
    fre = bre * h[0] - bim * h[1]
    fim = bre * h[1] + bim * h[0]
    f = jnp.concatenate([fre, fim], axis=-1).astype(jnp.bfloat16)
    g = dot(f, bf(mid.T), ((2,), (0,)))
    gre, gim = g[..., :tokens], g[..., tokens:]
    hre, him = gre * tc - gim * ts, gim * tc + gre * ts
    g = jnp.stack([hre, him]).astype(jnp.bfloat16).reshape(2 * rows, chans * tokens)
    y = dot(bf(back), g, ((1,), (0,)))
    return y.astype(jnp.bfloat16).reshape(groups, chans, tokens)


def local(query_branch, key_branch, value_branch, spectrum, skip_gain, out_weight):
    groups = lax.axis_size(CTX)
    tokens, channels = query_branch.shape
    chans = channels // groups
    mixed = (key_branch.astype(jnp.float32) * value_branch.astype(jnp.float32)).astype(
        jnp.bfloat16
    )
    mixed_t = mixed.T
    filt_t = spectrum.astype(jnp.bfloat16).transpose(3, 0, 1, 2).reshape(channels, -1)
    payload = jnp.concatenate([mixed_t, filt_t], axis=1).reshape(groups, -1)
    got = lax.all_to_all(payload, CTX, 0, 0, tiled=True).reshape(groups, chans, -1)
    signal = got[:, :, :tokens]
    filt = got[:, :, tokens:].reshape(groups, chans, *spectrum.shape[:3])
    y = convolve(signal, filt)
    y = lax.all_to_all(y.reshape(groups, -1), CTX, 0, 0, tiled=True).reshape(channels, tokens)
    gated = (
        query_branch.T.astype(jnp.float32)
        * (y.astype(jnp.float32) + skip_gain[:, None] * mixed_t.astype(jnp.float32))
    ).astype(jnp.bfloat16)
    part = dot(out_weight, gated, ((0,), (0,))).astype(jnp.bfloat16)
    summed = lax.psum_scatter(part, TP, scatter_dimension=0, tiled=True)
    return summed.astype(jnp.float32).T.astype(jnp.bfloat16)


def solution(mesh):
    fine = Mesh(mesh.devices.reshape(4, 4, 4, 4, 2), ("x", "zh", "y", "zl", "core"))
    placed = (
        P(CTX, TP),
        P(CTX, TP),
        P(CTX, TP),
        P(None, CTX, None, TP),
        P(TP),
        P(TP, None),
    )
    return jax.shard_map(local, mesh=fine, in_specs=placed, out_specs=P(CTX, TP), check_vma=False)
```

```python
import math

import jax
import jax.numpy as jnp
import numpy as np
from jax import lax
from jax.experimental import pallas as pl
from jax.experimental.pallas import tpu as pltpu
from jax.sharding import Mesh
from jax.sharding import PartitionSpec as P

CTX = ("x", "zh", "y")
LANES = 128
BLOCK = 256
CHANS = 4
TOKENS = 192
F32, BF16 = jnp.float32, jnp.bfloat16


def tables(groups):
    rows, length = 2 * groups, 2 * groups * TOKENS
    kb = (np.arange(2)[:, None] + 2 * np.arange(groups)[None, :]).reshape(-1)
    n1, n2 = np.arange(groups), np.arange(TOKENS)
    first = 2.0 * math.pi * (np.outer(kb, n1) % rows) / rows
    middle = 2.0 * math.pi * (np.outer(n2, n2) % TOKENS) / TOKENS
    turn = 2.0 * math.pi * (np.outer(kb, n2) % length) / length
    fwd = np.concatenate([np.cos(first), -np.sin(first)], axis=0)
    back = fwd.T / length
    pad = ((0, 0), (0, BLOCK - TOKENS))
    cos_m, sin_m = (np.pad(f(middle), (pad[1], pad[1])) for f in (np.cos, np.sin))
    mid = np.block([[cos_m, -sin_m], [sin_m, cos_m]])
    turn = np.stack([np.pad(np.cos(turn), pad), np.pad(np.sin(turn), pad)])
    return (
        jnp.asarray(fwd, BF16),
        jnp.asarray(back, BF16),
        jnp.asarray(mid, BF16),
        jnp.asarray(turn, F32),
    )


def dot(a, b, dims=((1,), (0,))):
    return lax.dot_general(a, b, (dims, ((), ())), preferred_element_type=F32)


def low_half(shape):
    return lax.broadcasted_iota(jnp.int32, shape, 0) % 8 < 4


def pack_kernel(k_ref, v_ref, h_ref, out_ref):
    mixed = (k_ref[...].astype(F32) * v_ref[...].astype(F32)).astype(BF16).astype(F32)
    half, rest = LANES, TOKENS - LANES

    def column(j):
        if j == 0:
            rows = mixed[:half]
        elif j == 1:
            rows = jnp.concatenate([mixed[half:], h_ref[3, pl.ds(0, rest), :]], axis=0)
        elif j % 2 == 0:
            rows = h_ref[j // 2 - 1, pl.ds(0, half), :]
        else:
            last = h_ref[j // 2 - 1, pl.ds(half, rest), :]
            more = (
                h_ref[3, pl.ds(rest * (j // 2), rest), :] if j < 7 else jnp.zeros_like(last)
            )
            rows = jnp.concatenate([last, more], axis=0)
        return rows.T

    for j in range(4):
        a, b = column(j), column(j + 4)
        channels = a.shape[0]
        low = low_half(a.shape)
        even = jnp.where(low, a, pltpu.roll(b, 4, axis=0))
        odd = jnp.where(low, pltpu.roll(a, channels - 4, axis=0), b)
        both = jnp.stack(
            [even.reshape(channels // 8, 8, LANES), odd.reshape(channels // 8, 8, LANES)], axis=1
        )
        out_ref[:, :, pl.ds(j * LANES, LANES)] = both.reshape(channels // 4, 8, LANES).astype(BF16)


def conv_kernel(got_ref, fwd_ref, back_ref, mid_ref, turn_ref, out_ref, wide_ref, flat_ref):
    groups = got_ref.shape[0]
    rows = 2 * groups
    for j in range(4):
        tiles = got_ref[:, :, pl.ds(j * LANES, LANES)].astype(F32)
        wide_ref[j] = tiles.reshape(8 * groups, LANES)
    lower = lax.broadcasted_iota(jnp.int32, (groups, LANES), 1) < TOKENS - LANES
    signal, filt = [], []
    for c in range(CHANS):
        x, h0, h1, h2 = (
            jnp.concatenate(
                [
                    wide_ref[2 * (block % 2) + j, pl.ds(first + c, groups, stride=8), :]
                    for j in range(2)
                ],
                axis=1,
            )
            for block, first in ((0, 0), (1, 0), (2, CHANS), (3, CHANS))
        )
        shift = LANES - (TOKENS - LANES)
        h3 = jnp.concatenate(
            [
                jnp.where(lower, pltpu.roll(x[:, LANES:], shift, axis=1), h0[:, LANES:]),
                pltpu.roll(h1[:, LANES:], shift, axis=1),
            ],
            axis=1,
        )
        signal.append(x)
        filt.append((jnp.concatenate([h0, h1], axis=0), jnp.concatenate([h2, h3], axis=0)))
    a = dot(fwd_ref[...], jnp.concatenate(signal, axis=1).astype(BF16))
    tc, ts = turn_ref[0], turn_ref[1]
    turned = []
    for c in range(CHANS):
        re, im = a[:rows, c * BLOCK : (c + 1) * BLOCK], a[rows:, c * BLOCK : (c + 1) * BLOCK]
        turned.append(jnp.concatenate([re * tc + im * ts, im * tc - re * ts], axis=1).astype(BF16))
    b = dot(jnp.concatenate(turned, axis=0), mid_ref[...])
    product = []
    for c in range(CHANS):
        re, im = b[c * rows : (c + 1) * rows, :BLOCK], b[c * rows : (c + 1) * rows, BLOCK:]
        hr, hi = filt[c]
        product.append(jnp.concatenate([re * hr - im * hi, re * hi + im * hr], axis=1).astype(BF16))
    g = dot(jnp.concatenate(product, axis=0), mid_ref[...], ((1,), (1,)))
    turned = []
    for c in range(CHANS):
        re, im = g[c * rows : (c + 1) * rows, :BLOCK], g[c * rows : (c + 1) * rows, BLOCK:]
        turned.append(jnp.concatenate([re * tc - im * ts, im * tc + re * ts], axis=0).astype(BF16))
    y = dot(back_ref[...], jnp.concatenate(turned, axis=1))
    for c in range(CHANS):
        for half in range(2):
            start = c * BLOCK + half * LANES
            flat_ref[pl.ds(half * CHANS + c, groups, stride=8), :] = y[:, start : start + LANES]
    out_ref[...] = flat_ref[...].astype(BF16).reshape(out_ref.shape)


def gate_kernel(got_ref, q_ref, k_ref, v_ref, skip_ref, out_ref):
    groups = got_ref.shape[0]
    tiles = got_ref[...].astype(F32).reshape(groups // 2, 2, 8, LANES)
    even = tiles[:, 0].reshape(4 * groups, LANES)
    odd = tiles[:, 1].reshape(4 * groups, LANES)
    low = low_half(even.shape)
    first = jnp.where(low, even, pltpu.roll(odd, 4, axis=0))
    second = jnp.where(low, pltpu.roll(even, 4 * groups - 4, axis=0), odd)
    conv = jnp.concatenate([first.T, second.T[: TOKENS - LANES]], axis=0)
    mixed = (k_ref[...].astype(F32) * v_ref[...].astype(F32)).astype(BF16).astype(F32)
    gated = q_ref[...].astype(F32) * (conv + skip_ref[...] * mixed)
    out_ref[...] = gated.astype(BF16)


def call(kernel, shape, args, scratch=()):
    return pl.pallas_call(
        kernel,
        out_shape=jax.ShapeDtypeStruct(shape, BF16),
        scratch_shapes=list(scratch),
        compiler_params=pltpu.CompilerParams(vmem_limit_bytes=40 * 2**20),
    )(*args)


def local(query_branch, key_branch, value_branch, spectrum, skip_gain, out_weight):
    groups = lax.axis_size(CTX)
    tokens, channels = query_branch.shape
    lines, cores = lax.axis_size("zl"), lax.axis_size("core")
    width = out_weight.shape[1] // (lines * cores)
    core = lax.axis_index("core")
    by_core = out_weight.reshape(channels, lines, cores, width)
    mine = lax.dynamic_index_in_dim(by_core, core, 2, keepdims=False)
    other = lax.dynamic_index_in_dim(by_core, 1 - core, 2, keepdims=False)
    other = lax.ppermute(other, "core", [(0, 1), (1, 0)])
    payload = call(
        pack_kernel,
        (groups, 8, 4 * LANES),
        (key_branch, value_branch, spectrum.reshape(4, tokens, channels)),
    )
    got = lax.all_to_all(payload, CTX, 0, 0, tiled=True)
    y = call(
        conv_kernel,
        (groups, 8, LANES),
        (got, *tables(groups)),
        [pltpu.VMEM((4, 8 * groups, LANES), F32), pltpu.VMEM((8 * groups, LANES), F32)],
    )
    y = lax.all_to_all(y, CTX, 0, 0, tiled=True)
    gated = call(
        gate_kernel,
        (tokens, channels),
        (y, query_branch, key_branch, value_branch, skip_gain.reshape(1, channels)),
    )
    near = lax.all_gather(gated, "core", axis=0)
    ours = lax.dynamic_index_in_dim(near, core, 0, keepdims=False)
    theirs = lax.dynamic_index_in_dim(near, 1 - core, 0, keepdims=False)
    dims = ((1,), (0,))
    part = dot(ours, mine, dims) + dot(theirs, other, dims)
    part = part.astype(BF16).transpose(1, 0, 2)
    part = lax.all_to_all(part, "zl", 0, 0, tiled=True)
    return jnp.sum(part.astype(F32), axis=0).astype(BF16)


def solution(mesh):
    fine = Mesh(mesh.devices.reshape(4, 4, 4, 4, 2), ("x", "zh", "y", "zl", "core"))
    tp = ("zl", "core")
    placed = (
        P(CTX, tp),
        P(CTX, tp),
        P(CTX, tp),
        P(None, CTX, None, tp),
        P(tp),
        P(tp, None),
    )
    return jax.shard_map(local, mesh=fine, in_specs=placed, out_specs=P(CTX, tp), check_vma=False)
```

```python
import math

import jax
import jax.numpy as jnp
import numpy as np
from jax import lax
from jax.experimental import pallas as pl
from jax.experimental.pallas import tpu as pltpu
from jax.sharding import Mesh
from jax.sharding import PartitionSpec as P

CTX = ("x", "zh", "y")
LANES = 128
BLOCK = 256
CHANS = 4
TOKENS = 192
F32, BF16 = jnp.float32, jnp.bfloat16


def tables(groups):
    rows, length = 2 * groups, 2 * groups * TOKENS
    kb = (np.arange(2)[:, None] + 2 * np.arange(groups)[None, :]).reshape(-1)
    n1, n2 = np.arange(groups), np.arange(TOKENS)
    first = 2.0 * math.pi * (np.outer(kb, n1) % rows) / rows
    middle = 2.0 * math.pi * (np.outer(n2, n2) % TOKENS) / TOKENS
    turn = 2.0 * math.pi * (np.outer(kb, n2) % length) / length
    fwd = np.concatenate([np.cos(first), -np.sin(first)], axis=0)
    back = fwd.T / length
    pad = ((0, 0), (0, BLOCK - TOKENS))
    cos_m, sin_m = (np.pad(f(middle), (pad[1], pad[1])) for f in (np.cos, np.sin))
    mid = np.block([[cos_m, -sin_m], [sin_m, cos_m]])
    turn = np.stack([np.pad(np.cos(turn), pad), np.pad(np.sin(turn), pad)])
    return (
        jnp.asarray(fwd, BF16),
        jnp.asarray(back, BF16),
        jnp.asarray(mid, BF16),
        jnp.asarray(turn, F32),
    )


def dot(a, b, dims=((1,), (0,))):
    return lax.dot_general(a, b, (dims, ((), ())), preferred_element_type=F32)


def low_half(shape):
    return lax.broadcasted_iota(jnp.int32, shape, 0) % 8 < 4


def pack_kernel(k_hbm, v_hbm, h_hbm, out_ref, k_ref, v_ref, h_ref, sems):
    pairs = ((k_hbm, k_ref), (v_hbm, v_ref), (h_hbm, h_ref))
    copies = [pltpu.make_async_copy(a, b, sems.at[i]) for i, (a, b) in enumerate(pairs)]
    for copy in copies:
        copy.start()
    for copy in copies:
        copy.wait()
    mixed = (k_ref[...].astype(F32) * v_ref[...].astype(F32)).astype(BF16).astype(F32)
    half, rest = LANES, TOKENS - LANES

    def column(j):
        if j == 0:
            rows = mixed[:half]
        elif j == 1:
            rows = jnp.concatenate([mixed[half:], h_ref[3, pl.ds(0, rest), :]], axis=0)
        elif j % 2 == 0:
            rows = h_ref[j // 2 - 1, pl.ds(0, half), :]
        else:
            last = h_ref[j // 2 - 1, pl.ds(half, rest), :]
            more = (
                h_ref[3, pl.ds(rest * (j // 2), rest), :] if j < 7 else jnp.zeros_like(last)
            )
            rows = jnp.concatenate([last, more], axis=0)
        return rows.T

    for j in range(4):
        a, b = column(j), column(j + 4)
        channels = a.shape[0]
        low = low_half(a.shape)
        even = jnp.where(low, a, pltpu.roll(b, 4, axis=0))
        odd = jnp.where(low, pltpu.roll(a, channels - 4, axis=0), b)
        both = jnp.stack(
            [even.reshape(channels // 8, 8, LANES), odd.reshape(channels // 8, 8, LANES)], axis=1
        )
        out_ref[:, :, pl.ds(j * LANES, LANES)] = both.reshape(channels // 4, 8, LANES).astype(BF16)


def conv_kernel(got_ref, fwd_ref, back_ref, mid_ref, turn_ref, out_ref, wide_ref, flat_ref):
    groups = got_ref.shape[0]
    rows = 2 * groups
    for j in range(4):
        tiles = got_ref[:, :, pl.ds(j * LANES, LANES)].astype(F32)
        wide_ref[j] = tiles.reshape(8 * groups, LANES)
    lower = lax.broadcasted_iota(jnp.int32, (groups, LANES), 1) < TOKENS - LANES
    signal, filt = [], []
    for c in range(CHANS):
        x, h0, h1, h2 = (
            jnp.concatenate(
                [
                    wide_ref[2 * (block % 2) + j, pl.ds(first + c, groups, stride=8), :]
                    for j in range(2)
                ],
                axis=1,
            )
            for block, first in ((0, 0), (1, 0), (2, CHANS), (3, CHANS))
        )
        shift = LANES - (TOKENS - LANES)
        h3 = jnp.concatenate(
            [
                jnp.where(lower, pltpu.roll(x[:, LANES:], shift, axis=1), h0[:, LANES:]),
                pltpu.roll(h1[:, LANES:], shift, axis=1),
            ],
            axis=1,
        )
        signal.append(x)
        filt.append((jnp.concatenate([h0, h1], axis=0), jnp.concatenate([h2, h3], axis=0)))
    a = dot(fwd_ref[...], jnp.concatenate(signal, axis=1).astype(BF16))
    tc, ts = turn_ref[0], turn_ref[1]
    turned = []
    for c in range(CHANS):
        re, im = a[:rows, c * BLOCK : (c + 1) * BLOCK], a[rows:, c * BLOCK : (c + 1) * BLOCK]
        turned.append(jnp.concatenate([re * tc + im * ts, im * tc - re * ts], axis=1).astype(BF16))
    b = dot(jnp.concatenate(turned, axis=0), mid_ref[...])
    product = []
    for c in range(CHANS):
        re, im = b[c * rows : (c + 1) * rows, :BLOCK], b[c * rows : (c + 1) * rows, BLOCK:]
        hr, hi = filt[c]
        product.append(jnp.concatenate([re * hr - im * hi, re * hi + im * hr], axis=1).astype(BF16))
    g = dot(jnp.concatenate(product, axis=0), mid_ref[...], ((1,), (1,)))
    turned = []
    for c in range(CHANS):
        re, im = g[c * rows : (c + 1) * rows, :BLOCK], g[c * rows : (c + 1) * rows, BLOCK:]
        turned.append(jnp.concatenate([re * tc - im * ts, im * tc + re * ts], axis=0).astype(BF16))
    y = dot(back_ref[...], jnp.concatenate(turned, axis=1))
    for c in range(CHANS):
        for half in range(2):
            start = c * BLOCK + half * LANES
            flat_ref[pl.ds(half * CHANS + c, groups, stride=8), :] = y[:, start : start + LANES]
    out_ref[...] = flat_ref[...].astype(BF16).reshape(out_ref.shape)


def gate_kernel(got_ref, q_ref, k_ref, v_ref, skip_ref, out_ref):
    groups = got_ref.shape[0]
    tiles = got_ref[...].astype(F32).reshape(groups // 2, 2, 8, LANES)
    even = tiles[:, 0].reshape(4 * groups, LANES)
    odd = tiles[:, 1].reshape(4 * groups, LANES)
    low = low_half(even.shape)
    first = jnp.where(low, even, pltpu.roll(odd, 4, axis=0))
    second = jnp.where(low, pltpu.roll(even, 4 * groups - 4, axis=0), odd)
    conv = jnp.concatenate([first.T, second.T[: TOKENS - LANES]], axis=0)
    mixed = (k_ref[...].astype(F32) * v_ref[...].astype(F32)).astype(BF16).astype(F32)
    gated = q_ref[...].astype(F32) * (conv + skip_ref[...] * mixed)
    out_ref[...] = gated.astype(BF16)


def split_kernel(w_hbm, mine_hbm, other_hbm, sems):
    core = lax.axis_index("core")
    lines, _, width = mine_hbm.shape
    copies = []
    for line in range(lines):
        for side, (out, owner) in enumerate(((mine_hbm, core), (other_hbm, 1 - core))):
            start = pl.multiple_of((2 * line + owner) * width, LANES)
            copies.append(
                pltpu.make_async_copy(
                    w_hbm.at[:, pl.ds(start, width)], out.at[line], sems.at[2 * line + side]
                )
            )
    for copy in copies:
        copy.start()
    for copy in copies:
        copy.wait()


def project_kernel(near_ref, mine_ref, other_ref, *outs):
    core, line = lax.axis_index("core"), lax.axis_index("zl")
    ours, theirs = near_ref[core], near_ref[1 - core]
    for d, out in enumerate(outs):
        dest = line ^ d
        out[...] = (dot(ours, mine_ref[dest]) + dot(theirs, other_ref[dest])).astype(BF16)


def call(kernel, shapes, args, scratch=(), hbm=False, hbm_out=False):
    many = isinstance(shapes, list)
    out_shape = [jax.ShapeDtypeStruct(s, BF16) for s in (shapes if many else [shapes])]
    extra = {}
    if not hbm:
        extra["compiler_params"] = pltpu.CompilerParams(vmem_limit_bytes=24 * 2**20)
    else:
        extra["in_specs"] = [pl.BlockSpec(memory_space=pltpu.HBM)] * len(args)
    if hbm_out:
        extra["out_specs"] = [pl.BlockSpec(memory_space=pl.ANY)] * len(out_shape)
    out = pl.pallas_call(
        kernel,
        out_shape=out_shape,
        scratch_shapes=list(scratch),
        **extra,
    )(*args)
    return out if many else out[0]


def local(query_branch, key_branch, value_branch, spectrum, skip_gain, out_weight):
    groups = lax.axis_size(CTX)
    tokens, channels = query_branch.shape
    lines, cores = lax.axis_size("zl"), lax.axis_size("core")
    width = out_weight.shape[1] // (lines * cores)
    payload = call(
        pack_kernel,
        (groups, 8, 4 * LANES),
        (key_branch, value_branch, spectrum.reshape(4, tokens, channels)),
        [
            pltpu.VMEM((tokens, channels), BF16),
            pltpu.VMEM((tokens, channels), BF16),
            pltpu.VMEM((4, tokens, channels), F32),
            pltpu.SemaphoreType.DMA((3,)),
        ],
        hbm=True,
    )
    got = lax.all_to_all(payload, CTX, 0, 0, tiled=True)
    mine, other = call(
        split_kernel,
        [(lines, channels, width)] * 2,
        (out_weight,),
        [pltpu.SemaphoreType.DMA((2 * lines,))],
        hbm=True,
        hbm_out=True,
    )
    other = lax.ppermute(other, "core", [(0, 1), (1, 0)])
    y = call(
        conv_kernel,
        (groups, 8, LANES),
        (got, *tables(groups)),
        [pltpu.VMEM((4, 8 * groups, LANES), F32), pltpu.VMEM((8 * groups, LANES), F32)],
    )
    y = lax.all_to_all(y, CTX, 0, 0, tiled=True)
    gated = call(
        gate_kernel,
        (tokens, channels),
        (y, query_branch, key_branch, value_branch, skip_gain.reshape(1, channels)),
    )
    near = lax.all_gather(gated, "core", axis=0)
    pieces = call(project_kernel, [(tokens, width)] * lines, (near, mine, other))
    total = pieces[0].astype(F32)
    for d in (3, 2, 1):
        back = lax.ppermute(pieces[d], "zl", [(i, i ^ d) for i in range(lines)])
        total = total + back.astype(F32)
    return total.astype(BF16)


def solution(mesh):
    fine = Mesh(mesh.devices.reshape(4, 4, 4, 4, 2), ("x", "zh", "y", "zl", "core"))
    tp = ("zl", "core")
    placed = (
        P(CTX, tp),
        P(CTX, tp),
        P(CTX, tp),
        P(None, CTX, None, tp),
        P(tp),
        P(tp, None),
    )
    return jax.shard_map(local, mesh=fine, in_specs=placed, out_specs=P(CTX, tp), check_vma=False)
```

```python
import math

import jax
import jax.numpy as jnp
import numpy as np
from jax import lax
from jax.experimental import pallas as pl
from jax.experimental.pallas import tpu as pltpu
from jax.sharding import Mesh
from jax.sharding import PartitionSpec as P

CTX = ("x", "zh", "y")
LANES = 128
BLOCK = 256
CHANS = 4
TOKENS = 192
F32, BF16 = jnp.float32, jnp.bfloat16


def tables(groups):
    rows, length = 2 * groups, 2 * groups * TOKENS
    kb = (np.arange(2)[:, None] + 2 * np.arange(groups)[None, :]).reshape(-1)
    n1, n2 = np.arange(groups), np.arange(TOKENS)
    first = 2.0 * math.pi * (np.outer(n1, kb) % rows) / rows
    middle = 2.0 * math.pi * (np.outer(n2, n2) % TOKENS) / TOKENS
    turn = 2.0 * math.pi * (np.outer(kb, n2) % length) / length
    ends = np.concatenate([np.cos(first), -np.sin(first)], axis=1)
    pad = ((0, 0), (0, BLOCK - TOKENS))
    cos_m, sin_m = (np.pad(f(middle), (pad[1], pad[1])) for f in (np.cos, np.sin))
    return jnp.asarray(
        np.concatenate(
            [
                np.block([[cos_m, -sin_m], [sin_m, cos_m]]),
                np.concatenate([np.pad(np.cos(turn), pad), np.pad(np.sin(turn), pad)], axis=1),
                np.concatenate([ends, ends / length], axis=1),
            ]
        ),
        BF16,
    )


def dot(a, b, dims=((1,), (0,))):
    return lax.dot_general(a, b, (dims, ((), ())), preferred_element_type=F32)


def low_half(shape):
    return lax.broadcasted_iota(jnp.int32, shape, 0) % 8 < 4


def pack_kernel(k_hbm, v_hbm, h_hbm, out_ref, mixed_ref, k_ref, v_ref, h_ref, sems):
    pairs = [(h_hbm.at[i], h_ref.at[i]) for i in range(4)] + [(k_hbm, k_ref), (v_hbm, v_ref)]
    copies = [pltpu.make_async_copy(a, b, sems.at[i]) for i, (a, b) in enumerate(pairs)]
    for i in (0, 2, 4, 5, 1, 3):
        copies[i].start()
    half, rest = LANES, TOKENS - LANES

    def column(j):
        if j == 0:
            rows = mixed_ref[pl.ds(0, half), :].astype(F32)
        elif j == 1:
            rows = jnp.concatenate(
                [mixed_ref[pl.ds(half, rest), :].astype(F32), h_ref[3, pl.ds(0, rest), :]], axis=0
            )
        elif j % 2 == 0:
            rows = h_ref[j // 2 - 1, pl.ds(0, half), :]
        else:
            last = h_ref[j // 2 - 1, pl.ds(half, rest), :]
            if j < 7:
                more = h_ref[3, pl.ds(rest * (j // 2), rest), :]
            else:
                more = pltpu.roll(last, last.shape[1] - 2, axis=1)
            rows = jnp.concatenate([last, more], axis=0)
        return rows.T

    def tile(j):
        a, b = column(j), column(j + 4)
        channels = a.shape[0]
        low = low_half(a.shape)
        even = jnp.where(low, a, pltpu.roll(b, 4, axis=0))
        odd = jnp.where(low, pltpu.roll(a, channels - 4, axis=0), b)
        both = jnp.stack(
            [even.reshape(channels // 8, 8, LANES), odd.reshape(channels // 8, 8, LANES)], axis=1
        )
        return both.reshape(channels // 4, 8, LANES)

    tiles = [None] * 4
    for j, needs in ((2, (0, 2)), (0, (4, 5, 1)), (1, (3,)), (3, ())):
        for i in needs:
            copies[i].wait()
        if j == 0:
            mixed_ref[...] = (k_ref[...].astype(F32) * v_ref[...].astype(F32)).astype(BF16)
        tiles[j] = tile(j)
    out_ref[...] = jnp.concatenate(tiles, axis=1)[:, : out_ref.shape[1]].astype(BF16)


def conv_kernel(got_ref, table_ref, out_ref, wide_ref, flat_ref):
    groups = got_ref.shape[0]
    rows = 2 * groups
    got = got_ref[...].astype(F32)
    for j in range(4):
        rows_j = got[:, 8 * j : 8 * j + 8]
        short = 8 - rows_j.shape[1]
        if short:
            rows_j = jnp.concatenate([rows_j, jnp.zeros((groups, short, LANES), F32)], axis=1)
        wide_ref[j] = rows_j.reshape(8 * groups, LANES)
    lower = lax.broadcasted_iota(jnp.int32, (groups, LANES), 1) < TOKENS - LANES
    shift = TOKENS - LANES

    def load(c, j):
        return wide_ref[j % 4, pl.ds(CHANS * (j // 4) + c, groups, stride=8), :]

    mid = table_ref[pl.ds(0, 2 * BLOCK), :]
    turn = table_ref[pl.ds(2 * BLOCK, rows), :].astype(F32)
    ends = table_ref[pl.ds(2 * BLOCK + rows, groups), :]
    tc, ts = turn[:, :BLOCK], turn[:, BLOCK:]
    signal, filt = [], []
    for c in range(CHANS):
        t = [load(c, j) for j in range(7)] + [load(c % 2, 7)]
        if c >= 2:
            t[7] = pltpu.roll(t[7], shift, axis=1)
        signal.append(jnp.concatenate([t[0], t[1]], axis=1))
        third = jnp.where(lower, pltpu.roll(t[1], shift, axis=1), t[3])
        hr = jnp.concatenate(
            [jnp.concatenate([t[2], t[3]], axis=1), jnp.concatenate([t[4], t[5]], axis=1)], axis=0
        )
        hi = jnp.concatenate(
            [
                jnp.concatenate([t[6], t[7]], axis=1),
                jnp.concatenate([third, pltpu.roll(t[5], shift, axis=1)], axis=1),
            ],
            axis=0,
        )
        filt.append((hr, hi))
    a = dot(ends[:, :BLOCK], jnp.concatenate(signal, axis=1).astype(BF16), ((0,), (0,)))
    turned = []
    for c in range(CHANS):
        re, im = a[:rows, c * BLOCK : (c + 1) * BLOCK], a[rows:, c * BLOCK : (c + 1) * BLOCK]
        turned.append(jnp.concatenate([re * tc + im * ts, im * tc - re * ts], axis=1).astype(BF16))
    b = dot(jnp.concatenate(turned, axis=0), mid)
    product = []
    for c in range(CHANS):
        re, im = b[c * rows : (c + 1) * rows, :BLOCK], b[c * rows : (c + 1) * rows, BLOCK:]
        hr, hi = filt[c]
        product.append(jnp.concatenate([re * hr - im * hi, re * hi + im * hr], axis=1).astype(BF16))
    g = dot(jnp.concatenate(product, axis=0), mid, ((1,), (1,)))
    turned = []
    for c in range(CHANS):
        re, im = g[c * rows : (c + 1) * rows, :BLOCK], g[c * rows : (c + 1) * rows, BLOCK:]
        turned.append(jnp.concatenate([re * tc - im * ts, im * tc + re * ts], axis=0).astype(BF16))
    y = dot(ends[:, BLOCK:], jnp.concatenate(turned, axis=1))
    for c in range(CHANS):
        flat_ref[pl.ds(c, groups, stride=8), :] = y[:, c * BLOCK : c * BLOCK + LANES]
    for c in range(2):
        one, two = (y[:, e * BLOCK + LANES : (e + 1) * BLOCK] for e in (c, c + 2))
        pair = jnp.where(lower, one, pltpu.roll(two, shift, axis=1))
        flat_ref[pl.ds(CHANS + c, groups, stride=8), :] = pair
        flat_ref[pl.ds(CHANS + 2 + c, groups, stride=8), :] = jnp.zeros_like(pair)
    out = flat_ref[...].reshape(groups, 8, LANES)
    out_ref[...] = out[:, : out_ref.shape[1]].astype(BF16)


def gate_kernel(got_ref, q_ref, mixed_ref, skip_ref, out_ref):
    groups, height, _ = got_ref.shape
    got = got_ref[...].astype(F32)
    got = jnp.concatenate([got, jnp.zeros((groups, 8 - height, LANES), F32)], axis=1)
    got = got.reshape(8 * groups, LANES)
    far = pltpu.roll(pltpu.roll(got, TOKENS - LANES, axis=1), 2, axis=0)
    row = lax.broadcasted_iota(jnp.int32, got.shape, 0) % 8
    tiles = jnp.where(row < 6, got, far).reshape(groups // 2, 2, 8, LANES)
    even = tiles[:, 0].reshape(4 * groups, LANES)
    odd = tiles[:, 1].reshape(4 * groups, LANES)
    low = low_half(even.shape)
    first = jnp.where(low, even, pltpu.roll(odd, 4, axis=0))
    second = jnp.where(low, pltpu.roll(even, 4 * groups - 4, axis=0), odd)
    conv = jnp.concatenate([first.T, second.T[: TOKENS - LANES]], axis=0)
    gated = q_ref[...].astype(F32) * (conv + skip_ref[...] * mixed_ref[...].astype(F32))
    out_ref[...] = gated.astype(BF16)


def split_kernel(w_hbm, mine_ref, other_ref, sems):
    core = lax.axis_index("core")
    lines, _, width = mine_ref.shape
    copies = []
    for line in range(lines):
        for side, (out, owner) in enumerate(((mine_ref, core), (other_ref, 1 - core))):
            start = pl.multiple_of((2 * line + owner) * width, LANES)
            copies.append(
                pltpu.make_async_copy(
                    w_hbm.at[:, pl.ds(start, width)], out.at[line], sems.at[2 * line + side]
                )
            )
    for copy in copies:
        copy.start()
    for copy in copies:
        copy.wait()


def project_kernel(near_ref, mine_ref, other_ref, out_ref):
    core = lax.axis_index("core")
    ours, theirs = near_ref[core], near_ref[1 - core]
    for dest in range(out_ref.shape[0]):
        out_ref[dest] = (dot(ours, mine_ref[dest]) + dot(theirs, other_ref[dest])).astype(BF16)


def call(kernel, shapes, args, scratch=(), hbm=False):
    many = isinstance(shapes, list)
    out_shape = [jax.ShapeDtypeStruct(s, BF16) for s in (shapes if many else [shapes])]
    extra = {}
    if not hbm:
        extra["compiler_params"] = pltpu.CompilerParams(vmem_limit_bytes=24 * 2**20)
    else:
        extra["in_specs"] = [pl.BlockSpec(memory_space=pltpu.HBM)] * len(args)
    out = pl.pallas_call(
        kernel,
        out_shape=out_shape,
        scratch_shapes=list(scratch),
        **extra,
    )(*args)
    return out if many else out[0]


def local(query_branch, key_branch, value_branch, spectrum, skip_gain, out_weight):
    groups = lax.axis_size(CTX)
    tokens, channels = query_branch.shape
    lines, cores = lax.axis_size("zl"), lax.axis_size("core")
    width = out_weight.shape[1] // (lines * cores)
    payload, mixed = call(
        pack_kernel,
        [(groups, 30, LANES), (tokens, channels)],
        (key_branch, value_branch, spectrum.reshape(4, tokens, channels)),
        [
            pltpu.VMEM((tokens, channels), BF16),
            pltpu.VMEM((tokens, channels), BF16),
            pltpu.VMEM((4, tokens, channels), F32),
            pltpu.SemaphoreType.DMA((6,)),
        ],
        hbm=True,
    )
    got = lax.all_to_all(payload, CTX, 0, 0, tiled=True)
    mine, other = call(
        split_kernel,
        [(lines, channels, width)] * 2,
        (out_weight,),
        [pltpu.SemaphoreType.DMA((2 * lines,))],
        hbm=True,
    )
    other = lax.ppermute(other, "core", [(0, 1), (1, 0)])
    y = call(
        conv_kernel,
        (groups, 6, LANES),
        (got, tables(groups)),
        [pltpu.VMEM((4, 8 * groups, LANES), F32), pltpu.VMEM((8 * groups, LANES), F32)],
    )
    y = lax.all_to_all(y, CTX, 0, 0, tiled=True)
    gated = call(
        gate_kernel,
        (tokens, channels),
        (y, query_branch, mixed, skip_gain.reshape(1, channels)),
    )
    near = lax.all_gather(gated, "core", axis=0)
    pieces = call(project_kernel, (lines, tokens, width), (near, mine, other))
    pieces = lax.all_to_all(pieces, "zl", 0, 0, tiled=True)
    return jnp.sum(pieces.astype(F32), axis=0).astype(BF16)


def solution(mesh):
    fine = Mesh(mesh.devices.reshape(4, 4, 4, 4, 2), ("x", "zh", "y", "zl", "core"))
    tp = ("zl", "core")
    placed = (
        P(CTX, tp),
        P(CTX, tp),
        P(CTX, tp),
        P(None, CTX, None, tp),
        P(tp),
        P(tp, None),
    )
    return jax.shard_map(local, mesh=fine, in_specs=placed, out_specs=P(CTX, tp), check_vma=False)
```

```python
import functools
import math

import jax
import jax.numpy as jnp
import numpy as np
from jax import lax
from jax.experimental import pallas as pl
from jax.experimental.pallas import tpu as pltpu
from jax.sharding import Mesh
from jax.sharding import PartitionSpec as P

CTX = ("x", "zh", "y")
LANES = 128
BLOCK = 256
CHANS = 4
TOKENS = 192
F32, BF16 = jnp.float32, jnp.bfloat16


def tables(groups):
    rows, length = 2 * groups, 2 * groups * TOKENS
    kb = (np.arange(2)[:, None] + 2 * np.arange(groups)[None, :]).reshape(-1)
    n1, n2 = np.arange(groups), np.arange(TOKENS)
    first = 2.0 * math.pi * (np.outer(n1, kb) % rows) / rows
    middle = 2.0 * math.pi * (np.outer(n2, n2) % TOKENS) / TOKENS
    turn = 2.0 * math.pi * (np.outer(kb, n2) % length) / length
    ends = np.concatenate([np.cos(first), -np.sin(first)], axis=1)
    pad = ((0, 0), (0, BLOCK - TOKENS))
    cos_m, sin_m = (np.pad(f(middle), (pad[1], pad[1])) for f in (np.cos, np.sin))
    return jnp.asarray(
        np.concatenate(
            [
                np.block([[cos_m, -sin_m], [sin_m, cos_m]]),
                np.concatenate([np.pad(np.cos(turn), pad), np.pad(np.sin(turn), pad)], axis=1),
                np.concatenate([ends, ends / length], axis=1),
            ]
        ),
        BF16,
    )


def dot(a, b, dims=((1,), (0,))):
    return lax.dot_general(a, b, (dims, ((), ())), preferred_element_type=F32)


def low_half(shape):
    return lax.broadcasted_iota(jnp.int32, shape, 0) % 8 < 4


def pack_kernel(k_hbm, v_hbm, h_hbm, out_ref, mixed_ref, k_ref, v_ref, h_ref, sems):
    pairs = [(h_hbm.at[i], h_ref.at[i]) for i in range(4)] + [(k_hbm, k_ref), (v_hbm, v_ref)]
    copies = [pltpu.make_async_copy(a, b, sems.at[i]) for i, (a, b) in enumerate(pairs)]
    for i in (0, 2, 4, 5, 1, 3):
        copies[i].start()
    half, rest = LANES, TOKENS - LANES

    def column(j):
        if j == 0:
            rows = mixed_ref[pl.ds(0, half), :].astype(F32)
        elif j == 1:
            rows = jnp.concatenate(
                [mixed_ref[pl.ds(half, rest), :].astype(F32), h_ref[3, pl.ds(0, rest), :]], axis=0
            )
        elif j % 2 == 0:
            rows = h_ref[j // 2 - 1, pl.ds(0, half), :]
        else:
            last = h_ref[j // 2 - 1, pl.ds(half, rest), :]
            if j < 7:
                more = h_ref[3, pl.ds(rest * (j // 2), rest), :]
            else:
                more = pltpu.roll(last, last.shape[1] - 2, axis=1)
            rows = jnp.concatenate([last, more], axis=0)
        return rows.T

    def tile(j):
        a, b = column(j), column(j + 4)
        channels = a.shape[0]
        low = low_half(a.shape)
        even = jnp.where(low, a, pltpu.roll(b, 4, axis=0))
        odd = jnp.where(low, pltpu.roll(a, channels - 4, axis=0), b)
        both = jnp.stack(
            [even.reshape(channels // 8, 8, LANES), odd.reshape(channels // 8, 8, LANES)], axis=1
        )
        return both.reshape(channels // 4, 8, LANES)

    tiles = [None] * 4
    for j, needs in ((2, (0, 2)), (0, (4, 5, 1)), (1, (3,)), (3, ())):
        for i in needs:
            copies[i].wait()
        if j == 0:
            mixed_ref[...] = (k_ref[...].astype(F32) * v_ref[...].astype(F32)).astype(BF16)
        tiles[j] = tile(j)
    out_ref[...] = jnp.concatenate(tiles, axis=1)[:, : out_ref.shape[1]].astype(BF16)


def conv_kernel(got_ref, table_ref, out_ref, wide_ref, flat_ref):
    groups = got_ref.shape[0]
    rows = 2 * groups
    got = got_ref[...].astype(F32)
    for j in range(4):
        rows_j = got[:, 8 * j : 8 * j + 8]
        short = 8 - rows_j.shape[1]
        if short:
            rows_j = jnp.concatenate([rows_j, jnp.zeros((groups, short, LANES), F32)], axis=1)
        wide_ref[j] = rows_j.reshape(8 * groups, LANES)
    lower = lax.broadcasted_iota(jnp.int32, (groups, LANES), 1) < TOKENS - LANES
    shift = TOKENS - LANES

    def load(c, j):
        return wide_ref[j % 4, pl.ds(CHANS * (j // 4) + c, groups, stride=8), :]

    mid = table_ref[pl.ds(0, 2 * BLOCK), :]
    turn = table_ref[pl.ds(2 * BLOCK, rows), :].astype(F32)
    ends = table_ref[pl.ds(2 * BLOCK + rows, groups), :]
    tc, ts = turn[:, :BLOCK], turn[:, BLOCK:]
    signal, filt = [], []
    for c in range(CHANS):
        t = [load(c, j) for j in range(7)] + [load(c % 2, 7)]
        if c >= 2:
            t[7] = pltpu.roll(t[7], shift, axis=1)
        signal.append(jnp.concatenate([t[0], t[1]], axis=1))
        third = jnp.where(lower, pltpu.roll(t[1], shift, axis=1), t[3])
        hr = jnp.concatenate(
            [jnp.concatenate([t[2], t[3]], axis=1), jnp.concatenate([t[4], t[5]], axis=1)], axis=0
        )
        hi = jnp.concatenate(
            [
                jnp.concatenate([t[6], t[7]], axis=1),
                jnp.concatenate([third, pltpu.roll(t[5], shift, axis=1)], axis=1),
            ],
            axis=0,
        )
        filt.append((hr, hi))
    a = dot(ends[:, :BLOCK], jnp.concatenate(signal, axis=1).astype(BF16), ((0,), (0,)))
    turned = []
    for c in range(CHANS):
        re, im = a[:rows, c * BLOCK : (c + 1) * BLOCK], a[rows:, c * BLOCK : (c + 1) * BLOCK]
        turned.append(jnp.concatenate([re * tc + im * ts, im * tc - re * ts], axis=1).astype(BF16))
    b = dot(jnp.concatenate(turned, axis=0), mid)
    product = []
    for c in range(CHANS):
        re, im = b[c * rows : (c + 1) * rows, :BLOCK], b[c * rows : (c + 1) * rows, BLOCK:]
        hr, hi = filt[c]
        product.append(jnp.concatenate([re * hr - im * hi, re * hi + im * hr], axis=1).astype(BF16))
    g = dot(jnp.concatenate(product, axis=0), mid, ((1,), (1,)))
    turned = []
    for c in range(CHANS):
        re, im = g[c * rows : (c + 1) * rows, :BLOCK], g[c * rows : (c + 1) * rows, BLOCK:]
        turned.append(jnp.concatenate([re * tc - im * ts, im * tc + re * ts], axis=0).astype(BF16))
    y = dot(ends[:, BLOCK:], jnp.concatenate(turned, axis=1))
    for c in range(CHANS):
        flat_ref[pl.ds(c, groups, stride=8), :] = y[:, c * BLOCK : c * BLOCK + LANES]
    for c in range(2):
        one, two = (y[:, e * BLOCK + LANES : (e + 1) * BLOCK] for e in (c, c + 2))
        pair = jnp.where(lower, one, pltpu.roll(two, shift, axis=1))
        flat_ref[pl.ds(CHANS + c, groups, stride=8), :] = pair
        flat_ref[pl.ds(CHANS + 2 + c, groups, stride=8), :] = jnp.zeros_like(pair)
    out = flat_ref[...].reshape(groups, 8, LANES)
    out_ref[...] = out[:, : out_ref.shape[1]].astype(BF16)


def gate_kernel(got_ref, q_ref, mixed_ref, skip_ref, out_ref):
    groups, height, _ = got_ref.shape
    got = got_ref[...].astype(F32)
    got = jnp.concatenate([got, jnp.zeros((groups, 8 - height, LANES), F32)], axis=1)
    got = got.reshape(8 * groups, LANES)
    far = pltpu.roll(pltpu.roll(got, TOKENS - LANES, axis=1), 2, axis=0)
    row = lax.broadcasted_iota(jnp.int32, got.shape, 0) % 8
    tiles = jnp.where(row < 6, got, far).reshape(groups // 2, 2, 8, LANES)
    even = tiles[:, 0].reshape(4 * groups, LANES)
    odd = tiles[:, 1].reshape(4 * groups, LANES)
    low = low_half(even.shape)
    first = jnp.where(low, even, pltpu.roll(odd, 4, axis=0))
    second = jnp.where(low, pltpu.roll(even, 4 * groups - 4, axis=0), odd)
    conv = jnp.concatenate([first.T, second.T[: TOKENS - LANES]], axis=0)
    gated = q_ref[...].astype(F32) * (conv + skip_ref[...] * mixed_ref[...].astype(F32))
    out_ref[...] = gated.astype(BF16)


def split_kernel(w_hbm, mine_ref, other_ref, sems):
    core = lax.axis_index("core")
    lines, _, width = mine_ref.shape
    copies = []
    for line in range(lines):
        for side, (out, owner) in enumerate(((mine_ref, core), (other_ref, 1 - core))):
            start = pl.multiple_of((2 * line + owner) * width, LANES)
            copies.append(
                pltpu.make_async_copy(
                    w_hbm.at[:, pl.ds(start, width)], out.at[line], sems.at[2 * line + side]
                )
            )
    for copy in copies:
        copy.start()
    for copy in copies:
        copy.wait()


def project_kernel(half, near_ref, mine_ref, other_ref, send_ref, keep_ref):
    core, line = lax.axis_index("core"), lax.axis_index("zl")
    ours, theirs = near_ref[core], near_ref[1 - core]
    width = send_ref.shape[-1]
    columns = pl.ds(half * width, width)
    for d, out in ((1, send_ref.at[0]), (3, send_ref.at[1]), (2, keep_ref.at[1]), (0, keep_ref.at[0])):
        dest = line ^ d
        total = dot(ours, mine_ref[dest, :, columns]) + dot(theirs, other_ref[dest, :, columns])
        out[...] = total.astype(BF16)


def finish_kernel(*refs):
    out_ref = refs[-1]
    halves = [refs[i : i + 3] for i in range(0, len(refs) - 1, 3)]
    for half, (keep, back, far) in enumerate(halves):
        total = keep[0].astype(F32) + back[0].astype(F32) + far[...].astype(F32)
        out_ref[:, pl.ds(half * far.shape[1], far.shape[1])] = total.astype(BF16)


def call(kernel, shapes, args, scratch=(), hbm=False):
    many = isinstance(shapes, list)
    out_shape = [jax.ShapeDtypeStruct(s, BF16) for s in (shapes if many else [shapes])]
    extra = {}
    if not hbm:
        extra["compiler_params"] = pltpu.CompilerParams(vmem_limit_bytes=24 * 2**20)
    else:
        extra["in_specs"] = [pl.BlockSpec(memory_space=pltpu.HBM)] * len(args)
    out = pl.pallas_call(
        kernel,
        out_shape=out_shape,
        scratch_shapes=list(scratch),
        **extra,
    )(*args)
    return out if many else out[0]


def local(query_branch, key_branch, value_branch, spectrum, skip_gain, out_weight):
    groups = lax.axis_size(CTX)
    tokens, channels = query_branch.shape
    lines, cores = lax.axis_size("zl"), lax.axis_size("core")
    width = out_weight.shape[1] // (lines * cores)
    payload, mixed = call(
        pack_kernel,
        [(groups, 30, LANES), (tokens, channels)],
        (key_branch, value_branch, spectrum.reshape(4, tokens, channels)),
        [
            pltpu.VMEM((tokens, channels), BF16),
            pltpu.VMEM((tokens, channels), BF16),
            pltpu.VMEM((4, tokens, channels), F32),
            pltpu.SemaphoreType.DMA((6,)),
        ],
        hbm=True,
    )
    got = lax.all_to_all(payload, CTX, 0, 0, tiled=True)
    mine, other = call(
        split_kernel,
        [(lines, channels, width)] * 2,
        (out_weight,),
        [pltpu.SemaphoreType.DMA((2 * lines,))],
        hbm=True,
    )
    other = lax.ppermute(other, "core", [(0, 1), (1, 0)])
    y = call(
        conv_kernel,
        (groups, 6, LANES),
        (got, tables(groups)),
        [pltpu.VMEM((4, 8 * groups, LANES), F32), pltpu.VMEM((8 * groups, LANES), F32)],
    )
    y = lax.all_to_all(y, CTX, 0, 0, tiled=True)
    gated = call(
        gate_kernel,
        (tokens, channels),
        (y, query_branch, mixed, skip_gain.reshape(1, channels)),
    )
    near = lax.all_gather(gated, "core", axis=0)
    def trade(value, d):
        return lax.ppermute(value, "zl", [(i, i ^ d) for i in range(lines)])

    parts = 2
    shape = (2, tokens, width // parts)
    first = []
    for half in range(parts):
        send, keep = call(
            functools.partial(project_kernel, half), [shape, shape], (near, mine, other)
        )
        first.append((keep, trade(send, 1)))
    shares = []
    for keep, back in first:
        far = (keep[1].astype(F32) + back[1].astype(F32)).astype(BF16)
        shares += [keep, back, trade(far, 2)]
    return call(finish_kernel, (tokens, width), shares)


def solution(mesh):
    fine = Mesh(mesh.devices.reshape(4, 4, 4, 4, 2), ("x", "zh", "y", "zl", "core"))
    tp = ("zl", "core")
    placed = (
        P(CTX, tp),
        P(CTX, tp),
        P(CTX, tp),
        P(None, CTX, None, tp),
        P(tp),
        P(tp, None),
    )
    return jax.shard_map(local, mesh=fine, in_specs=placed, out_specs=P(CTX, tp), check_vma=False)
```

```python
import functools
import math

import jax
import jax.numpy as jnp
import numpy as np
from jax import lax
from jax.experimental import pallas as pl
from jax.experimental.pallas import tpu as pltpu
from jax.sharding import Mesh
from jax.sharding import PartitionSpec as P

CTX = "ctx"
FIRST = 42
LANES = 128
BLOCK = 256
CHANS = 4
TOKENS = 192
F32, BF16 = jnp.float32, jnp.bfloat16


def order(groups):
    return [(FIRST + rank) % groups for rank in range(groups)]


def tables(groups):
    rows, length = 2 * groups, 2 * groups * TOKENS
    n1, n2 = np.array(order(groups)), np.arange(TOKENS)
    kb = (np.arange(2)[:, None] + 2 * n1[None, :]).reshape(-1)
    first = 2.0 * math.pi * (np.outer(n1, kb) % rows) / rows
    middle = 2.0 * math.pi * (np.outer(n2, n2) % TOKENS) / TOKENS
    turn = 2.0 * math.pi * (np.outer(kb, n2) % length) / length
    ends = np.concatenate([np.cos(first), -np.sin(first)], axis=1)
    pad = ((0, 0), (0, BLOCK - TOKENS))
    cos_m, sin_m = (np.pad(f(middle), (pad[1], pad[1])) for f in (np.cos, np.sin))
    return jnp.asarray(
        np.concatenate(
            [
                np.block([[cos_m, -sin_m], [sin_m, cos_m]]),
                np.concatenate([np.pad(np.cos(turn), pad), np.pad(np.sin(turn), pad)], axis=1),
                np.concatenate([ends, ends / length], axis=1),
            ]
        ),
        BF16,
    )


def dot(a, b, dims=((1,), (0,))):
    return lax.dot_general(a, b, (dims, ((), ())), preferred_element_type=F32)


def low_half(shape):
    return lax.broadcasted_iota(jnp.int32, shape, 0) % 8 < 4


def pack_kernel(k_hbm, v_hbm, h_hbm, out_ref, mixed_ref, k_ref, v_ref, h_ref, sems):
    pairs = [(h_hbm.at[i], h_ref.at[i]) for i in range(4)] + [(k_hbm, k_ref), (v_hbm, v_ref)]
    copies = [pltpu.make_async_copy(a, b, sems.at[i]) for i, (a, b) in enumerate(pairs)]
    for i in (0, 2, 4, 5, 1, 3):
        copies[i].start()
    half, rest = LANES, TOKENS - LANES

    def column(j):
        if j == 0:
            rows = mixed_ref[pl.ds(0, half), :].astype(F32)
        elif j == 1:
            rows = jnp.concatenate(
                [mixed_ref[pl.ds(half, rest), :].astype(F32), h_ref[3, pl.ds(0, rest), :]], axis=0
            )
        elif j % 2 == 0:
            rows = h_ref[j // 2 - 1, pl.ds(0, half), :]
        else:
            last = h_ref[j // 2 - 1, pl.ds(half, rest), :]
            if j < 7:
                more = h_ref[3, pl.ds(rest * (j // 2), rest), :]
            else:
                more = pltpu.roll(last, last.shape[1] - 2, axis=1)
            rows = jnp.concatenate([last, more], axis=0)
        return rows.T

    def tile(j):
        a, b = column(j), column(j + 4)
        channels = a.shape[0]
        low = low_half(a.shape)
        even = jnp.where(low, a, pltpu.roll(b, 4, axis=0))
        odd = jnp.where(low, pltpu.roll(a, channels - 4, axis=0), b)
        both = jnp.stack(
            [even.reshape(channels // 8, 8, LANES), odd.reshape(channels // 8, 8, LANES)], axis=1
        )
        return both.reshape(channels // 4, 8, LANES)

    tiles = [None] * 4
    for j, needs in ((2, (0, 2)), (0, (4, 5, 1)), (1, (3,)), (3, ())):
        for i in needs:
            copies[i].wait()
        if j == 0:
            mixed_ref[...] = (k_ref[...].astype(F32) * v_ref[...].astype(F32)).astype(BF16)
        tiles[j] = tile(j)
    out_ref[...] = jnp.concatenate(tiles, axis=1)[:, : out_ref.shape[1]].astype(BF16)


def conv_kernel(got_ref, table_ref, out_ref, wide_ref, flat_ref):
    groups = got_ref.shape[0]
    rows = 2 * groups
    got = got_ref[...].astype(F32)
    for j in range(4):
        rows_j = got[:, 8 * j : 8 * j + 8]
        short = 8 - rows_j.shape[1]
        if short:
            rows_j = jnp.concatenate([rows_j, jnp.zeros((groups, short, LANES), F32)], axis=1)
        wide_ref[j] = rows_j.reshape(8 * groups, LANES)
    lower = lax.broadcasted_iota(jnp.int32, (groups, LANES), 1) < TOKENS - LANES
    shift = TOKENS - LANES

    def load(c, j):
        return wide_ref[j % 4, pl.ds(CHANS * (j // 4) + c, groups, stride=8), :]

    mid = table_ref[pl.ds(0, 2 * BLOCK), :]
    turn = table_ref[pl.ds(2 * BLOCK, rows), :].astype(F32)
    ends = table_ref[pl.ds(2 * BLOCK + rows, groups), :]
    tc, ts = turn[:, :BLOCK], turn[:, BLOCK:]
    signal, filt = [], []
    for c in range(CHANS):
        t = [load(c, j) for j in range(7)] + [load(c % 2, 7)]
        if c >= 2:
            t[7] = pltpu.roll(t[7], shift, axis=1)
        signal.append(jnp.concatenate([t[0], t[1]], axis=1))
        third = jnp.where(lower, pltpu.roll(t[1], shift, axis=1), t[3])
        hr = jnp.concatenate(
            [jnp.concatenate([t[2], t[3]], axis=1), jnp.concatenate([t[4], t[5]], axis=1)], axis=0
        )
        hi = jnp.concatenate(
            [
                jnp.concatenate([t[6], t[7]], axis=1),
                jnp.concatenate([third, pltpu.roll(t[5], shift, axis=1)], axis=1),
            ],
            axis=0,
        )
        filt.append((hr, hi))
    a = dot(ends[:, :BLOCK], jnp.concatenate(signal, axis=1).astype(BF16), ((0,), (0,)))
    turned = []
    for c in range(CHANS):
        re, im = a[:rows, c * BLOCK : (c + 1) * BLOCK], a[rows:, c * BLOCK : (c + 1) * BLOCK]
        turned.append(jnp.concatenate([re * tc + im * ts, im * tc - re * ts], axis=1).astype(BF16))
    b = dot(jnp.concatenate(turned, axis=0), mid)
    product = []
    for c in range(CHANS):
        re, im = b[c * rows : (c + 1) * rows, :BLOCK], b[c * rows : (c + 1) * rows, BLOCK:]
        hr, hi = filt[c]
        product.append(jnp.concatenate([re * hr - im * hi, re * hi + im * hr], axis=1).astype(BF16))
    g = dot(jnp.concatenate(product, axis=0), mid, ((1,), (1,)))
    turned = []
    for c in range(CHANS):
        re, im = g[c * rows : (c + 1) * rows, :BLOCK], g[c * rows : (c + 1) * rows, BLOCK:]
        turned.append(jnp.concatenate([re * tc - im * ts, im * tc + re * ts], axis=0).astype(BF16))
    y = dot(ends[:, BLOCK:], jnp.concatenate(turned, axis=1))
    for c in range(CHANS):
        flat_ref[pl.ds(c, groups, stride=8), :] = y[:, c * BLOCK : c * BLOCK + LANES]
    for c in range(2):
        one, two = (y[:, e * BLOCK + LANES : (e + 1) * BLOCK] for e in (c, c + 2))
        pair = jnp.where(lower, one, pltpu.roll(two, shift, axis=1))
        flat_ref[pl.ds(CHANS + c, groups, stride=8), :] = pair
        flat_ref[pl.ds(CHANS + 2 + c, groups, stride=8), :] = jnp.zeros_like(pair)
    out = flat_ref[...].reshape(groups, 8, LANES)
    out_ref[...] = out[:, : out_ref.shape[1]].astype(BF16)


def gate_kernel(got_ref, q_ref, mixed_ref, skip_ref, out_ref):
    groups, height, _ = got_ref.shape
    got = got_ref[...].astype(F32)
    got = jnp.concatenate([got, jnp.zeros((groups, 8 - height, LANES), F32)], axis=1)
    got = got.reshape(8 * groups, LANES)
    far = pltpu.roll(pltpu.roll(got, TOKENS - LANES, axis=1), 2, axis=0)
    row = lax.broadcasted_iota(jnp.int32, got.shape, 0) % 8
    tiles = jnp.where(row < 6, got, far).reshape(groups // 2, 2, 8, LANES)
    even = tiles[:, 0].reshape(4 * groups, LANES)
    odd = tiles[:, 1].reshape(4 * groups, LANES)
    low = low_half(even.shape)
    first = jnp.where(low, even, pltpu.roll(odd, 4, axis=0))
    second = jnp.where(low, pltpu.roll(even, 4 * groups - 4, axis=0), odd)
    conv = jnp.concatenate([first.T, second.T[: TOKENS - LANES]], axis=0)
    gated = q_ref[...].astype(F32) * (conv + skip_ref[...] * mixed_ref[...].astype(F32))
    out_ref[...] = gated.astype(BF16)


def split_kernel(w_hbm, mine_ref, other_ref, sems):
    core = lax.axis_index("core")
    lines, _, width = mine_ref.shape
    copies = []
    for line in range(lines):
        for side, (out, owner) in enumerate(((mine_ref, core), (other_ref, 1 - core))):
            start = pl.multiple_of((2 * line + owner) * width, LANES)
            copies.append(
                pltpu.make_async_copy(
                    w_hbm.at[:, pl.ds(start, width)], out.at[line], sems.at[2 * line + side]
                )
            )
    for copy in copies:
        copy.start()
    for copy in copies:
        copy.wait()


def project_kernel(half, near_ref, mine_ref, other_ref, send_ref, keep_ref):
    core, line = lax.axis_index("core"), lax.axis_index("zl")
    ours, theirs = near_ref[core], near_ref[1 - core]
    width = send_ref.shape[-1]
    columns = pl.ds(half * width, width)
    for d, out in ((1, send_ref.at[0]), (3, send_ref.at[1]), (2, keep_ref.at[1]), (0, keep_ref.at[0])):
        dest = line ^ d
        total = dot(ours, mine_ref[dest, :, columns]) + dot(theirs, other_ref[dest, :, columns])
        out[...] = total.astype(BF16)


def finish_kernel(*refs):
    out_ref = refs[-1]
    halves = [refs[i : i + 3] for i in range(0, len(refs) - 1, 3)]
    for half, (keep, back, far) in enumerate(halves):
        total = keep[0].astype(F32) + back[0].astype(F32) + far[...].astype(F32)
        out_ref[:, pl.ds(half * far.shape[1], far.shape[1])] = total.astype(BF16)


def call(kernel, shapes, args, scratch=(), hbm=False):
    many = isinstance(shapes, list)
    out_shape = [jax.ShapeDtypeStruct(s, BF16) for s in (shapes if many else [shapes])]
    extra = {}
    if not hbm:
        extra["compiler_params"] = pltpu.CompilerParams(vmem_limit_bytes=24 * 2**20)
    else:
        extra["in_specs"] = [pl.BlockSpec(memory_space=pltpu.HBM)] * len(args)
    out = pl.pallas_call(
        kernel,
        out_shape=out_shape,
        scratch_shapes=list(scratch),
        **extra,
    )(*args)
    return out if many else out[0]


def exchange(value):
    groups = [order(lax.axis_size(CTX))]
    return lax.all_to_all(value, CTX, 0, 0, axis_index_groups=groups, tiled=True)


def local(query_branch, key_branch, value_branch, spectrum, skip_gain, out_weight):
    groups = lax.axis_size(CTX)
    tokens, channels = query_branch.shape
    lines, cores = lax.axis_size("zl"), lax.axis_size("core")
    width = out_weight.shape[1] // (lines * cores)
    payload, mixed = call(
        pack_kernel,
        [(groups, 30, LANES), (tokens, channels)],
        (key_branch, value_branch, spectrum.reshape(4, tokens, channels)),
        [
            pltpu.VMEM((tokens, channels), BF16),
            pltpu.VMEM((tokens, channels), BF16),
            pltpu.VMEM((4, tokens, channels), F32),
            pltpu.SemaphoreType.DMA((6,)),
        ],
        hbm=True,
    )
    got = exchange(payload)
    mine, other = call(
        split_kernel,
        [(lines, channels, width)] * 2,
        (out_weight,),
        [pltpu.SemaphoreType.DMA((2 * lines,))],
        hbm=True,
    )
    other = lax.ppermute(other, "core", [(0, 1), (1, 0)])
    y = call(
        conv_kernel,
        (groups, 6, LANES),
        (got, tables(groups)),
        [pltpu.VMEM((4, 8 * groups, LANES), F32), pltpu.VMEM((8 * groups, LANES), F32)],
    )
    y = exchange(y)
    gated = call(
        gate_kernel,
        (tokens, channels),
        (y, query_branch, mixed, skip_gain.reshape(1, channels)),
    )
    near = lax.all_gather(gated, "core", axis=0)
    def trade(value, d):
        return lax.ppermute(value, "zl", [(i, i ^ d) for i in range(lines)])

    parts = 2
    shape = (2, tokens, width // parts)
    first = []
    for half in range(parts):
        send, keep = call(
            functools.partial(project_kernel, half), [shape, shape], (near, mine, other)
        )
        first.append((keep, trade(send, 1)))
    shares = []
    for keep, back in first:
        far = (keep[1].astype(F32) + back[1].astype(F32)).astype(BF16)
        shares += [keep, back, trade(far, 2)]
    return call(finish_kernel, (tokens, width), shares)


def solution(mesh):
    fine = Mesh(mesh.devices.reshape(64, 4, 2), ("ctx", "zl", "core"))
    tp = ("zl", "core")
    placed = (
        P(CTX, tp),
        P(CTX, tp),
        P(CTX, tp),
        P(None, CTX, None, tp),
        P(tp),
        P(tp, None),
    )
    return jax.shard_map(local, mesh=fine, in_specs=placed, out_specs=P(CTX, tp), check_vma=False)
```

```python
import functools
import math

import jax
import jax.numpy as jnp
import numpy as np
from jax import lax
from jax.experimental import pallas as pl
from jax.experimental.pallas import tpu as pltpu
from jax.sharding import Mesh
from jax.sharding import PartitionSpec as P

CTX = "ctx"
FIRST = 42
LANES = 128
BLOCK = 256
CHANS = 4
TOKENS = 192
F32, BF16 = jnp.float32, jnp.bfloat16


def order(groups):
    return [(FIRST + rank) % groups for rank in range(groups)]


def tables(groups):
    rows, length = 2 * groups, 2 * groups * TOKENS
    n1, n2 = np.array(order(groups)), np.arange(TOKENS)
    kb = (np.arange(2)[:, None] + 2 * n1[None, :]).reshape(-1)
    first = 2.0 * math.pi * (np.outer(n1, kb) % rows) / rows
    middle = 2.0 * math.pi * (np.outer(n2, n2) % TOKENS) / TOKENS
    turn = 2.0 * math.pi * (np.outer(kb, n2) % length) / length
    ends = np.concatenate([np.cos(first), -np.sin(first)], axis=1)
    pad = ((0, 0), (0, BLOCK - TOKENS))
    cos_m, sin_m = (np.pad(f(middle), (pad[1], pad[1])) for f in (np.cos, np.sin))
    return jnp.asarray(
        np.concatenate(
            [
                np.block([[cos_m, -sin_m], [sin_m, cos_m]]),
                np.concatenate([np.pad(np.cos(turn), pad), np.pad(np.sin(turn), pad)], axis=1),
                np.concatenate([ends, ends / length], axis=1),
            ]
        ),
        BF16,
    )


def dot(a, b, dims=((1,), (0,))):
    return lax.dot_general(a, b, (dims, ((), ())), preferred_element_type=F32)


def low_half(shape):
    return lax.broadcasted_iota(jnp.int32, shape, 0) % 8 < 4


def pack_kernel(k_hbm, v_hbm, h_hbm, out_ref, mixed_ref, k_ref, v_ref, h_ref, sems):
    pairs = [(h_hbm.at[i], h_ref.at[i]) for i in range(4)] + [(k_hbm, k_ref), (v_hbm, v_ref)]
    copies = [pltpu.make_async_copy(a, b, sems.at[i]) for i, (a, b) in enumerate(pairs)]
    for i in (0, 2, 4, 5, 1, 3):
        copies[i].start()
    half, rest = LANES, TOKENS - LANES

    def column(j):
        if j == 0:
            rows = mixed_ref[pl.ds(0, half), :].astype(F32)
        elif j == 1:
            rows = jnp.concatenate(
                [mixed_ref[pl.ds(half, rest), :].astype(F32), h_ref[3, pl.ds(0, rest), :]], axis=0
            )
        elif j % 2 == 0:
            rows = h_ref[j // 2 - 1, pl.ds(0, half), :]
        else:
            last = h_ref[j // 2 - 1, pl.ds(half, rest), :]
            if j < 7:
                more = h_ref[3, pl.ds(rest * (j // 2), rest), :]
            else:
                more = pltpu.roll(last, last.shape[1] - 2, axis=1)
            rows = jnp.concatenate([last, more], axis=0)
        return rows.T

    def tile(j):
        a, b = column(j), column(j + 4)
        channels = a.shape[0]
        low = low_half(a.shape)
        even = jnp.where(low, a, pltpu.roll(b, 4, axis=0))
        odd = jnp.where(low, pltpu.roll(a, channels - 4, axis=0), b)
        both = jnp.stack(
            [even.reshape(channels // 8, 8, LANES), odd.reshape(channels // 8, 8, LANES)], axis=1
        )
        return both.reshape(channels // 4, 8, LANES)

    tiles = [None] * 4
    for j, needs in ((2, (0, 2)), (0, (4, 5, 1)), (1, (3,)), (3, ())):
        for i in needs:
            copies[i].wait()
        if j == 0:
            mixed_ref[...] = (k_ref[...].astype(F32) * v_ref[...].astype(F32)).astype(BF16)
        tiles[j] = tile(j)
    out_ref[...] = jnp.concatenate(tiles, axis=1)[:, : out_ref.shape[1]].astype(BF16)


def conv_kernel(got_ref, table_ref, out_ref, wide_ref, flat_ref):
    groups = got_ref.shape[0]
    rows = 2 * groups
    got = got_ref[...].astype(F32)
    for j in range(4):
        rows_j = got[:, 8 * j : 8 * j + 8]
        short = 8 - rows_j.shape[1]
        if short:
            rows_j = jnp.concatenate([rows_j, jnp.zeros((groups, short, LANES), F32)], axis=1)
        wide_ref[j] = rows_j.reshape(8 * groups, LANES)
    lower = lax.broadcasted_iota(jnp.int32, (groups, LANES), 1) < TOKENS - LANES
    shift = TOKENS - LANES

    def load(c, j):
        return wide_ref[j % 4, pl.ds(CHANS * (j // 4) + c, groups, stride=8), :]

    mid = table_ref[pl.ds(0, 2 * BLOCK), :]
    turn = table_ref[pl.ds(2 * BLOCK, rows), :].astype(F32)
    ends = table_ref[pl.ds(2 * BLOCK + rows, groups), :]
    tc, ts = turn[:, :BLOCK], turn[:, BLOCK:]
    signal, filt = [], []
    for c in range(CHANS):
        t = [load(c, j) for j in range(7)] + [load(c % 2, 7)]
        if c >= 2:
            t[7] = pltpu.roll(t[7], shift, axis=1)
        signal.append(jnp.concatenate([t[0], t[1]], axis=1))
        third = jnp.where(lower, pltpu.roll(t[1], shift, axis=1), t[3])
        hr = jnp.concatenate(
            [jnp.concatenate([t[2], t[3]], axis=1), jnp.concatenate([t[4], t[5]], axis=1)], axis=0
        )
        hi = jnp.concatenate(
            [
                jnp.concatenate([t[6], t[7]], axis=1),
                jnp.concatenate([third, pltpu.roll(t[5], shift, axis=1)], axis=1),
            ],
            axis=0,
        )
        filt.append((hr, hi))
    a = dot(ends[:, :BLOCK], jnp.concatenate(signal, axis=1).astype(BF16), ((0,), (0,)))
    turned = []
    for c in range(CHANS):
        re, im = a[:rows, c * BLOCK : (c + 1) * BLOCK], a[rows:, c * BLOCK : (c + 1) * BLOCK]
        turned.append(jnp.concatenate([re * tc + im * ts, im * tc - re * ts], axis=1).astype(BF16))
    b = dot(jnp.concatenate(turned, axis=0), mid)
    product = []
    for c in range(CHANS):
        re, im = b[c * rows : (c + 1) * rows, :BLOCK], b[c * rows : (c + 1) * rows, BLOCK:]
        hr, hi = filt[c]
        product.append(jnp.concatenate([re * hr - im * hi, re * hi + im * hr], axis=1).astype(BF16))
    g = dot(jnp.concatenate(product, axis=0), mid, ((1,), (1,)))
    turned = []
    for c in range(CHANS):
        re, im = g[c * rows : (c + 1) * rows, :BLOCK], g[c * rows : (c + 1) * rows, BLOCK:]
        turned.append(jnp.concatenate([re * tc - im * ts, im * tc + re * ts], axis=0).astype(BF16))
    y = dot(ends[:, BLOCK:], jnp.concatenate(turned, axis=1))
    for c in range(CHANS):
        flat_ref[pl.ds(c, groups, stride=8), :] = y[:, c * BLOCK : c * BLOCK + LANES]
    for c in range(2):
        one, two = (y[:, e * BLOCK + LANES : (e + 1) * BLOCK] for e in (c, c + 2))
        pair = jnp.where(lower, one, pltpu.roll(two, shift, axis=1))
        flat_ref[pl.ds(CHANS + c, groups, stride=8), :] = pair
        flat_ref[pl.ds(CHANS + 2 + c, groups, stride=8), :] = jnp.zeros_like(pair)
    out = flat_ref[...].reshape(groups, 8, LANES)
    out_ref[...] = out[:, : out_ref.shape[1]].astype(BF16)


def gate_kernel(got_ref, q_ref, mixed_ref, skip_ref, out_ref):
    groups, height, _ = got_ref.shape
    got = got_ref[...].astype(F32)
    got = jnp.concatenate([got, jnp.zeros((groups, 8 - height, LANES), F32)], axis=1)
    got = got.reshape(8 * groups, LANES)
    far = pltpu.roll(pltpu.roll(got, TOKENS - LANES, axis=1), 2, axis=0)
    row = lax.broadcasted_iota(jnp.int32, got.shape, 0) % 8
    tiles = jnp.where(row < 6, got, far).reshape(groups // 2, 2, 8, LANES)
    even = tiles[:, 0].reshape(4 * groups, LANES)
    odd = tiles[:, 1].reshape(4 * groups, LANES)
    low = low_half(even.shape)
    first = jnp.where(low, even, pltpu.roll(odd, 4, axis=0))
    second = jnp.where(low, pltpu.roll(even, 4 * groups - 4, axis=0), odd)
    conv = jnp.concatenate([first.T, second.T[: TOKENS - LANES]], axis=0)
    gated = q_ref[...].astype(F32) * (conv + skip_ref[...] * mixed_ref[...].astype(F32))
    out_ref[...] = gated.astype(BF16)


def split_kernel(w_hbm, mine_ref, other_ref, sems):
    core = lax.axis_index("core")
    lines, _, width = mine_ref.shape
    copies = []
    for line in range(lines):
        for side, (out, owner) in enumerate(((mine_ref, core), (other_ref, 1 - core))):
            start = pl.multiple_of((2 * line + owner) * width, LANES)
            copies.append(
                pltpu.make_async_copy(
                    w_hbm.at[:, pl.ds(start, width)], out.at[line], sems.at[2 * line + side]
                )
            )
    for copy in copies:
        copy.start()
    for copy in copies:
        copy.wait()


def project_kernel(half, away, near_ref, mine_ref, other_ref, out_ref):
    core, line = lax.axis_index("core"), lax.axis_index("zl")
    ours, theirs = near_ref[core], near_ref[1 - core]
    width = out_ref.shape[-1]
    columns = pl.ds(half * width, width)
    for i, d in enumerate(away):
        dest = line ^ d
        total = dot(ours, mine_ref[dest, :, columns]) + dot(theirs, other_ref[dest, :, columns])
        out_ref[i] = total.astype(BF16)


def finish_kernel(*refs):
    out_ref = refs[-1]
    halves = [refs[i : i + 3] for i in range(0, len(refs) - 1, 3)]
    for half, (keep, back, far) in enumerate(halves):
        total = keep[0].astype(F32) + back[0].astype(F32) + far[...].astype(F32)
        out_ref[:, pl.ds(half * far.shape[1], far.shape[1])] = total.astype(BF16)


def call(kernel, shapes, args, scratch=(), hbm=False):
    many = isinstance(shapes, list)
    out_shape = [jax.ShapeDtypeStruct(s, BF16) for s in (shapes if many else [shapes])]
    extra = {}
    if not hbm:
        extra["compiler_params"] = pltpu.CompilerParams(vmem_limit_bytes=24 * 2**20)
    else:
        extra["in_specs"] = [pl.BlockSpec(memory_space=pltpu.HBM)] * len(args)
    out = pl.pallas_call(
        kernel,
        out_shape=out_shape,
        scratch_shapes=list(scratch),
        **extra,
    )(*args)
    return out if many else out[0]


def exchange(value):
    groups = [order(lax.axis_size(CTX))]
    return lax.all_to_all(value, CTX, 0, 0, axis_index_groups=groups, tiled=True)


def local(query_branch, key_branch, value_branch, spectrum, skip_gain, out_weight):
    groups = lax.axis_size(CTX)
    tokens, channels = query_branch.shape
    lines, cores = lax.axis_size("zl"), lax.axis_size("core")
    width = out_weight.shape[1] // (lines * cores)
    payload, mixed = call(
        pack_kernel,
        [(groups, 30, LANES), (tokens, channels)],
        (key_branch, value_branch, spectrum.reshape(4, tokens, channels)),
        [
            pltpu.VMEM((tokens, channels), BF16),
            pltpu.VMEM((tokens, channels), BF16),
            pltpu.VMEM((4, tokens, channels), F32),
            pltpu.SemaphoreType.DMA((6,)),
        ],
        hbm=True,
    )
    got = exchange(payload)
    mine, other = call(
        split_kernel,
        [(lines, channels, width)] * 2,
        (out_weight,),
        [pltpu.SemaphoreType.DMA((2 * lines,))],
        hbm=True,
    )
    other = lax.ppermute(other, "core", [(0, 1), (1, 0)])
    y = call(
        conv_kernel,
        (groups, 6, LANES),
        (got, tables(groups)),
        [pltpu.VMEM((4, 8 * groups, LANES), F32), pltpu.VMEM((8 * groups, LANES), F32)],
    )
    y = exchange(y)
    gated = call(
        gate_kernel,
        (tokens, channels),
        (y, query_branch, mixed, skip_gain.reshape(1, channels)),
    )
    near = lax.all_gather(gated, "core", axis=0)
    def trade(value, d):
        return lax.ppermute(value, "zl", [(i, i ^ d) for i in range(lines)])

    parts = 2
    shape = (2, tokens, width // parts)
    def project(half, away):
        kernel = functools.partial(project_kernel, half, away)
        return call(kernel, shape, (near, mine, other))

    backs = [trade(project(half, (1, 3)), 1) for half in range(parts)]
    first = [(project(half, (0, 2)), back) for half, back in enumerate(backs)]
    shares = []
    for keep, back in first:
        far = (keep[1].astype(F32) + back[1].astype(F32)).astype(BF16)
        shares += [keep, back, trade(far, 2)]
    return call(finish_kernel, (tokens, width), shares)


def solution(mesh):
    fine = Mesh(mesh.devices.reshape(64, 4, 2), ("ctx", "zl", "core"))
    tp = ("zl", "core")
    placed = (
        P(CTX, tp),
        P(CTX, tp),
        P(CTX, tp),
        P(None, CTX, None, tp),
        P(tp),
        P(tp, None),
    )
    return jax.shard_map(local, mesh=fine, in_specs=placed, out_specs=P(CTX, tp), check_vma=False)
```
